32 devices in a mesh: space: 16 (over z, y, core), mem: 2 (over x).
Axes of the slice: x: 2, y: 2, z: 4, core: 2. Of those that a mesh axis runs over, the one named last changes fastest.
Arguments:
- state: float32 [64, 262144], P('mem', 'space'), may hold values from -6 to 6
- obs_index: int32 [4, 4096], P(None, 'space'), may hold values from 0 to 262143, as said below
- obs_value: float32 [4, 4096], P(None, 'space'), may hold values from -8 to 8
- obs_var: float32 [4, 4096], P(None, 'space'), may hold values from 0.02 to 5
Outputs:
- posterior: float32 [64, 262144], P('mem', 'space')
The draws below stay inside these ranges and needn't reach their ends.
Inputs may be any that keep to these rules, and one draw needn't show every extreme that they name: `obs_index`: observation k of every batch measures a column of the block owned by index k // 256 of space, that is a column between (k // 256) * 16384 and (k // 256 + 1) * 16384 - 1.
All inputs are finite; a program needn't handle non-finite values.
Results may differ from the reference program's by a relative error of at most 0.0075.
Values may be sent and summed in bfloat16 or wider, within the bound.
A program may use at most 64 MiB of HBM per device.

```python
import math
import jax
import jax.numpy as jnp
from jax import lax

M = 64
COLS = 16384
OBS_DEV = 256
BATCHES = 4
STATE = 262144
OBS = 4096
RADIUS = 32768
N_SPACE = 16


def draw_obs_index(key, part):
    blocks = OBS // OBS_DEV
    key_kind, key_place, key_offset = jax.random.split(key, 3)
    scattered = jax.random.randint(key_kind, (BATCHES, blocks), 0, 4, dtype=jnp.int32) == 0
    window = jnp.where(scattered, COLS, 2 * OBS_DEV).astype(jnp.int32)
    window_start = jax.random.randint(key_place, (BATCHES, blocks), 0, 1 << 30, dtype=jnp.int32) % (COLS - window + 1)
    window_full = jnp.repeat(window, OBS_DEV, axis=1)
    start_full = jnp.repeat(window_start, OBS_DEV, axis=1)
    raw_offset = jax.random.randint(key_offset, (BATCHES, OBS), 0, 1 << 30, dtype=jnp.int32)
    offsets = start_full + raw_offset % window_full
    owners = jnp.arange(OBS, dtype=jnp.int32) // OBS_DEV
    slot_index = jnp.arange(OBS, dtype=jnp.int32)[None, :]
    offsets = jnp.where(slot_index == 0, 0, offsets)
    offsets = jnp.where(slot_index == OBS - 1, COLS - 1, offsets)
    return (owners[None, :] * COLS + offsets).astype(jnp.int32)


def draw_obs_var(key, part):
    key_phase, key_level = jax.random.split(key)
    owners = jnp.arange(OBS, dtype=jnp.int32) // OBS_DEV
    phase = jax.random.randint(key_phase, (BATCHES, 1), 0, 4, dtype=jnp.int32)
    precise = (owners[None, :] + phase) % 4 == 0
    fraction = jax.random.uniform(key_level, (BATCHES, OBS), jnp.float32)
    sharp = 0.02 * jnp.exp(fraction * math.log(5.0))
    loose = jnp.exp(fraction * math.log(5.0))
    return jnp.where(precise, sharp, loose).astype(jnp.float32)


def level_of(stream_key, dims, pieces, low, high):
    level = 1.0
    for position, shards_of in pieces:
        heights = jax.random.uniform(jax.random.fold_in(jax.random.fold_in(stream_key, 6), position), (shards_of,), jnp.float32, low / len(pieces), high / len(pieces))
        level = level * jnp.repeat(jnp.exp(heights), dims[position] // shards_of).reshape((-1,) + (1,) * (len(dims) - 1 - position))
    return level


def scatter_about(stream_key, extent, scale, most, cuts=(), held_as=jnp.bfloat16):
    drawn = jax.random.normal(stream_key, extent, jnp.float32) * scale
    if len(cuts) > 0:
        drawn = level_of(stream_key, extent, cuts, -0.22, 0.18) * drawn
    return jnp.clip(drawn, min=-most, max=most).astype(held_as)


def setup_inputs(seed: int = 0) -> dict:
    streams_of = jax.random.split(jax.random.key(seed), 5)
    state = scatter_about(streams_of[0], (M, STATE), 1.0, 6.0, ((0, 2), (1, 16)), jnp.float32)
    obs_index = draw_obs_index(jax.random.fold_in(streams_of[4], 71), 0)
    obs_value = scatter_about(streams_of[2], (BATCHES, OBS), 1.5, 8.0, ((1, 16),), jnp.float32)
    obs_var = draw_obs_var(jax.random.fold_in(streams_of[4], 71), 0)
    return {"state": state, "obs_index": obs_index, "obs_value": obs_value, "obs_var": obs_var}


def summarize(prior_obs, values, variances):
    members = prior_obs.shape[0]
    obs_mean = lax.optimization_barrier(jnp.mean(prior_obs, axis=0))
    anomaly = prior_obs - obs_mean
    spread = lax.optimization_barrier(jnp.sum(anomaly * anomaly, axis=0)) / (members - 1) + 1e-06
    post_var = 1.0 / (1.0 / spread + 1.0 / variances)
    post_mean = post_var * (obs_mean / spread + values / variances)
    change = post_mean - obs_mean + (jnp.sqrt(post_var / spread) - 1.0) * anomaly
    weighted = (change / ((members - 1) * spread)).astype(jnp.bfloat16)
    return (anomaly.astype(jnp.bfloat16), weighted)

def reference(state, obs_index, obs_value, obs_var):
    members = state.shape[0]
    current = state
    margin = 2 * OBS_DEV
    for batch in range(BATCHES):
        positions = obs_index[batch]
        prior_obs = current[:, positions]
        anomaly, weighted = summarize(prior_obs, obs_value[batch], obs_var[batch])
        anomaly_pad = jnp.pad(anomaly, ((0, 0), (margin, margin)))
        weighted_pad = jnp.pad(weighted, ((0, 0), (margin, margin)))
        position_pad = jnp.pad(positions, (margin, margin))
        state_anom = (current - lax.optimization_barrier(jnp.mean(current, axis=0))).astype(jnp.bfloat16)
        spread_blocks = jnp.transpose(state_anom.reshape(members, N_SPACE, COLS), (1, 0, 2))

        def one_block(inputs):
            column_block, spread_piece = inputs
            band_start = (column_block * OBS_DEV).astype(jnp.int32)
            band_anom = lax.dynamic_slice_in_dim(anomaly_pad, band_start, 5 * OBS_DEV, 1)
            band_weight = lax.dynamic_slice_in_dim(weighted_pad, band_start, 5 * OBS_DEV, 1)
            band_pos = lax.dynamic_slice_in_dim(position_pad, band_start, 5 * OBS_DEV, 0)
            cov = jnp.dot(band_anom.T, spread_piece, preferred_element_type=jnp.float32)
            column_pos = (column_block * COLS).astype(jnp.int32) + lax.iota(jnp.int32, COLS)
            distance = jnp.abs(column_pos[None, :] - band_pos[:, None]).astype(jnp.float32)
            taper = jnp.square(jnp.maximum(0.0, 1.0 - distance / RADIUS))
            gain = (taper * cov).astype(jnp.bfloat16)
            return jnp.dot(band_weight, gain, preferred_element_type=jnp.float32)
        deltas = lax.map(one_block, (jnp.arange(N_SPACE, dtype=jnp.int32), spread_blocks))
        current = current + jnp.transpose(deltas, (1, 0, 2)).reshape(members, N_SPACE * COLS)
    return current
```

```python
import functools

import jax
import jax.numpy as jnp
from jax import lax
from jax.experimental import pallas as pl
from jax.experimental.pallas import tpu as pltpu
from jax.sharding import PartitionSpec as P

RADIUS = 32768
OFFSETS = (-2, 2, -1, 1)
SLOT = {-2: 0, 0: 1, 2: 2, -1: 3, 1: 4}
CHUNK = 256
f32, bf16 = jnp.float32, jnp.bfloat16


def gather_kernel(idx_ref, state_ref, out_ref):
    half_members, cols = state_ref.shape
    batches, obs_dev = idx_ref.shape
    base = lax.axis_index("space") * cols
    lanes = lax.broadcasted_iota(jnp.int32, (half_members, 128), 1)
    for batch in range(batches):
        for part in range(obs_dev // 128):
            def pick(step, acc):
                for inner in range(8):
                    t = step * 8 + inner
                    col = idx_ref[batch, part * 128 + t] - base
                    hi = lax.shift_right_logical(col, 7)
                    lo = col & 127
                    tile = state_ref[:, pl.ds(pl.multiple_of(hi * 128, 128), 128)]
                    moved = pltpu.roll(tile, (t - lo) & 127, 1)
                    acc = jnp.where(lanes == t, moved, acc)
                return acc
            at = batch * obs_dev + part * 128
            out_ref[:, at:at + 128] = lax.fori_loop(
                0, 16, pick, jnp.zeros((half_members, 128), f32))


def kernel(
    n_space, batches, obs_dev, half_members, cols,
    g_send, state_ref, pos_ref, value_ref, var_ref, out_ref,
    g_recv, g_ref, x_send, x_recv, cur, e_send, e_recv,
    pos_own, pos_nb, aw, a_t, coef, moment,
    g_sems, x_sems, e_sems, pos_ssem, pos_rsem, aw_ssem, aw_rsem,
):
    space = lax.axis_index("space")
    mem = lax.axis_index("mem")
    other = 1 - mem
    width = cols // 2
    members = 2 * half_members
    own_start = mem * width
    other_start = other * width
    base = space * cols
    block = cols / RADIUS
    partner = {"mem": other}
    valid = {o: (space + o >= 0) & (space + o < n_space) for o in OFFSETS}

    barrier = pltpu.get_barrier_semaphore()
    pl.semaphore_signal(barrier, inc=1, device_id=partner, device_id_type=pl.DeviceIdType.MESH)
    for o in OFFSETS:
        @pl.when(valid[o])
        def _(o=o):
            pl.semaphore_signal(
                barrier, inc=1, device_id={"space": space + o},
                device_id_type=pl.DeviceIdType.MESH)

    def g_copy(part):
        span = pl.ds(0, obs_dev) if part == 0 else pl.ds(obs_dev, (batches - 1) * obs_dev)
        return pltpu.make_async_remote_copy(
            src_ref=g_send.at[:, span], dst_ref=g_recv.at[:, span],
            send_sem=g_sems.at[0, part], recv_sem=g_sems.at[1, part],
            device_id=partner, device_id_type=pl.DeviceIdType.MESH)

    x_copy = pltpu.make_async_remote_copy(
        src_ref=x_send, dst_ref=x_recv, send_sem=x_sems.at[0], recv_sem=x_sems.at[1],
        device_id=partner, device_id_type=pl.DeviceIdType.MESH)

    groups = 8
    group_width = width // groups

    def e_copy(group):
        span = pl.ds(pl.multiple_of(group * group_width, 128), group_width)
        return pltpu.make_async_remote_copy(
            src_ref=e_send.at[:, span], dst_ref=e_recv.at[:, span],
            send_sem=e_sems.at[0, group], recv_sem=e_sems.at[1, group],
            device_id=partner, device_id_type=pl.DeviceIdType.MESH)

    def pos_copy(o):
        i = OFFSETS.index(o)
        back = OFFSETS.index(-o)
        return pltpu.make_async_remote_copy(
            src_ref=pos_own, dst_ref=pos_nb.at[back],
            send_sem=pos_ssem.at[i], recv_sem=pos_rsem.at[back],
            device_id={"space": space + o}, device_id_type=pl.DeviceIdType.MESH)

    def pos_wait(o):
        i = OFFSETS.index(o)
        pltpu.make_async_remote_copy(
            src_ref=pos_own, dst_ref=pos_nb.at[i],
            send_sem=pos_ssem.at[i], recv_sem=pos_rsem.at[i],
            device_id={"space": space + o}, device_id_type=pl.DeviceIdType.MESH).wait_recv()

    def aw_copy(batch, o):
        i = OFFSETS.index(o)
        back = OFFSETS.index(-o)
        return pltpu.make_async_remote_copy(
            src_ref=aw.at[batch, SLOT[0]], dst_ref=aw.at[batch, SLOT[-o]],
            send_sem=aw_ssem.at[batch, i], recv_sem=aw_rsem.at[batch, back],
            device_id={"space": space + o}, device_id_type=pl.DeviceIdType.MESH)

    def aw_wait(batch, o):
        i = OFFSETS.index(o)
        pltpu.make_async_remote_copy(
            src_ref=aw.at[batch, SLOT[0]], dst_ref=aw.at[batch, SLOT[o]],
            send_sem=aw_ssem.at[batch, i], recv_sem=aw_rsem.at[batch, i],
            device_id={"space": space + o}, device_id_type=pl.DeviceIdType.MESH).wait_recv()

    pos_own[...] = jnp.zeros_like(pos_own)
    pos_own[:batches, :] = (pos_ref[...] - base - cols // 2).astype(f32) * (1.0 / RADIUS)
    for o in OFFSETS:
        @pl.when(jnp.logical_not(valid[o]))
        def _(o=o):
            pos_nb[OFFSETS.index(o)] = jnp.zeros(pos_nb.shape[1:], f32)
            for batch in range(batches):
                aw[batch, SLOT[o]] = jnp.zeros(aw.shape[2:], bf16)

    count = 1
    for o in OFFSETS:
        count = count + jnp.where(valid[o], 1, 0)
    pl.semaphore_wait(barrier, count)
    g_copy(0).start()
    for o in OFFSETS:
        @pl.when(valid[o])
        def _(o=o):
            pos_copy(o).start()

    def cast(i, carry):
        at = pl.multiple_of(i * 1024, 128)
        x_send[:, pl.ds(at, 1024)] = state_ref[
            :, pl.ds(pl.multiple_of(other_start + at, 128), 1024)].astype(bf16)
        cur[:half_members, pl.ds(at, 1024)] = state_ref[
            :, pl.ds(pl.multiple_of(own_start + at, 128), 1024)]
        return carry
    lax.fori_loop(0, width // 1024, cast, 0)
    x_copy.start()
    g_copy(1).start()
    g_ref[:half_members, :] = g_send[...]

    def increment(batch, now, u):
        mean = jnp.sum(now, axis=0, keepdims=True) * (1.0 / members)
        anomaly = now - mean
        spread = anomaly.astype(bf16)
        total = jnp.dot(
            moment[:, :3 * members],
            jnp.concatenate(
                [spread, (anomaly * u).astype(bf16), (anomaly * (u * u)).astype(bf16)], axis=0),
            preferred_element_type=f32)
        for slot in range(3):
            cov = jnp.dot(
                a_t[slot * obs_dev:(slot + 1) * obs_dev, :], spread, preferred_element_type=f32)
            c = coef[slot]
            if slot == 0:
                t = jnp.maximum(c - u, 0.0)
            elif slot == 1:
                t = jnp.maximum(1.0 - jnp.abs(c - u), 0.0)
            else:
                t = jnp.maximum(c + u, 0.0)
            gain = (t * t * cov).astype(bf16)
            total = total + jnp.dot(
                aw[batch, slot, members:2 * members, :], gain, preferred_element_type=f32)
        return total

    def build(batch):
        def row(o):
            if o == 0:
                return pos_own[batch:batch + 1, :]
            return pos_nb[OFFSETS.index(o), batch:batch + 1, :] + o * block
        for o in (-2, 0, 2):
            slot = SLOT[o]
            q = row(o)
            c = q if o == 0 else (1.0 + q if o < 0 else 1.0 - q)
            coef[slot] = jnp.transpose(jnp.broadcast_to(c, (CHUNK, obs_dev)))
            a_t[slot * obs_dev:(slot + 1) * obs_dev, :] = jnp.transpose(
                aw[batch, slot, :members, :].astype(f32)).astype(bf16)
        sums = 0.0
        for o in (-1, 1):
            slot = SLOT[o]
            q = row(o)
            c = 1.0 + q if o < 0 else 1.0 - q
            a = aw[batch, slot, :members, :].astype(f32)
            rhs = jnp.concatenate([a * (c * c), a * (2.0 * o * c), a], axis=0).astype(bf16)
            sums = sums + lax.dot_general(
                aw[batch, slot, members:2 * members, :], rhs, (((1,), (1,)), ((), ())),
                preferred_element_type=f32)
        moment[:, :3 * members] = sums.astype(bf16)

    lane_u = lax.broadcasted_iota(jnp.int32, (1, CHUNK), 1)

    def chunk_update(batch, at):
        now = cur[:, pl.ds(at, CHUNK)]
        u = (lane_u + (own_start + at - cols // 2)).astype(f32) * (1.0 / RADIUS)
        return now + increment(batch, now, u)

    def full_update(batch):
        def step(i, carry):
            at = pl.multiple_of(i * CHUNK, CHUNK)
            cur[:, pl.ds(at, CHUNK)] = chunk_update(batch, at)
            return carry
        lax.fori_loop(0, width // CHUNK, step, 0)

    def last_update(batch):
        per = group_width // CHUNK

        def group_step(group, carry):
            def step(i, inner):
                at = pl.multiple_of((group * per + i) * CHUNK, CHUNK)
                done = chunk_update(batch, at)
                out_ref[:, pl.ds(pl.multiple_of(own_start + at, CHUNK), CHUNK)] = done[:half_members]
                e_send[:, pl.ds(at, CHUNK)] = (
                    done[half_members:] - x_recv[:, pl.ds(at, CHUNK)].astype(f32)).astype(bf16)
                return inner
            lax.fori_loop(0, per, step, 0)
            e_copy(group).start()
            return carry
        lax.fori_loop(0, groups, group_step, 0)

    def summarize(batch):
        span = slice(batch * obs_dev, (batch + 1) * obs_dev)
        prior = g_ref[:, span]
        values = value_ref[batch:batch + 1, :]
        variances = var_ref[batch:batch + 1, :]
        obs_mean = jnp.sum(prior, axis=0, keepdims=True) * (1.0 / members)
        anomaly = prior - obs_mean
        spread = jnp.sum(anomaly * anomaly, axis=0, keepdims=True) * (1.0 / (members - 1)) + 1e-06
        post_var = 1.0 / (1.0 / spread + 1.0 / variances)
        post_mean = post_var * (obs_mean / spread + values / variances)
        change = post_mean - obs_mean + (jnp.sqrt(post_var / spread) - 1.0) * anomaly
        aw[batch, SLOT[0], :members, :] = anomaly.astype(bf16)
        aw[batch, SLOT[0], members:, :] = (change / ((members - 1) * spread)).astype(bf16)

    for batch in range(batches):
        if batch == 0:
            g_copy(0).wait_recv()
            g_ref[half_members:, :obs_dev] = g_recv[:, :obs_dev]
        summarize(batch)
        for o in OFFSETS:
            @pl.when(valid[o])
            def _(o=o):
                aw_copy(batch, o).start()
        if batch == 0:
            g_copy(1).wait_recv()
            g_ref[half_members:, obs_dev:] = g_recv[:, obs_dev:]
            for o in OFFSETS:
                @pl.when(valid[o])
                def _(o=o):
                    pos_wait(o)
        else:
            if batch == 1:
                x_copy.wait_recv()

                def widen(i, carry):
                    at = pl.multiple_of(i * 1024, 128)
                    cur[half_members:, pl.ds(at, 1024)] = x_recv[:, pl.ds(at, 1024)].astype(f32)
                    return carry
                lax.fori_loop(0, width // 1024, widen, 0)
            full_update(batch - 1)
        for o in OFFSETS:
            @pl.when(valid[o])
            def _(o=o):
                aw_wait(batch, o)
        build(batch)
        for later in range(batch + 1, batches):
            span = slice(later * obs_dev, (later + 1) * obs_dev)
            now = g_ref[:, span]
            g_ref[:, span] = now + increment(batch, now, pos_own[later:later + 1, :])
    last_update(batches - 1)

    def finish(group, carry):
        e_copy(group).wait_recv()
        at = pl.multiple_of(group * group_width, 128)
        there = pl.ds(pl.multiple_of(other_start + at, 128), group_width)
        out_ref[:, there] = state_ref[:, there] + e_recv[:, pl.ds(at, group_width)].astype(f32)
        return carry
    lax.fori_loop(0, groups, finish, 0)

    g_copy(0).wait_send()
    g_copy(1).wait_send()
    x_copy.wait_send()
    lax.fori_loop(0, groups, lambda g, c: (e_copy(g).wait_send(), c)[1], 0)
    for o in OFFSETS:
        @pl.when(valid[o])
        def _(o=o):
            pos_copy(o).wait_send()
            for batch in range(batches):
                aw_copy(batch, o).wait_send()


def shards(n_space, state, obs_index, obs_value, obs_var):
    half_members, cols = state.shape
    batches, obs_dev = obs_index.shape
    members, width = 2 * half_members, cols // 2
    vmem = pl.BlockSpec(memory_space=pltpu.VMEM)
    smem = pl.BlockSpec(memory_space=pltpu.SMEM)
    n_obs = batches * obs_dev
    dma = pltpu.SemaphoreType.DMA
    flops = 4 * batches * members * (3 * obs_dev + 192) * width
    gathered = pl.pallas_call(
        gather_kernel,
        out_shape=jax.ShapeDtypeStruct((half_members, n_obs), f32),
        in_specs=[smem, vmem],
        out_specs=vmem,
        compiler_params=pltpu.CompilerParams(vmem_limit_bytes=32 * 1024 * 1024),
    )(obs_index, state)
    return pl.pallas_call(
        functools.partial(kernel, n_space, batches, obs_dev, half_members, cols),
        out_shape=jax.ShapeDtypeStruct(state.shape, f32),
        in_specs=[vmem, vmem, vmem, vmem, vmem],
        out_specs=vmem,
        scratch_shapes=[
            pltpu.VMEM((half_members, n_obs), f32),
            pltpu.VMEM((members, n_obs), f32),
            pltpu.VMEM((half_members, width), bf16),
            pltpu.VMEM((half_members, width), bf16),
            pltpu.VMEM((members, width), f32),
            pltpu.VMEM((half_members, width), bf16),
            pltpu.VMEM((half_members, width), bf16),
            pltpu.VMEM((8, obs_dev), f32),
            pltpu.VMEM((4, 8, obs_dev), f32),
            pltpu.VMEM((batches, 5, 2 * members, obs_dev), bf16),
            pltpu.VMEM((3 * obs_dev, members), bf16),
            pltpu.VMEM((3, obs_dev, CHUNK), f32),
            pltpu.VMEM((members, 256), bf16),
            dma((2, 2)), dma((2,)), dma((2, 8)), dma((4,)), dma((4,)),
            dma((batches, 4)), dma((batches, 4)),
        ],
        compiler_params=pltpu.CompilerParams(
            collective_id=0, has_side_effects=True, vmem_limit_bytes=48 * 1024 * 1024),
        cost_estimate=pl.CostEstimate(
            flops=flops, bytes_accessed=2 * state.size * 4, transcendentals=n_obs),
    )(gathered, state, obs_index, obs_value, obs_var)


def solution(mesh):
    placed = (P("mem", "space"), P(None, "space"), P(None, "space"), P(None, "space"))
    return jax.shard_map(
        functools.partial(shards, mesh.shape["space"]), mesh=mesh, in_specs=placed,
        out_specs=P("mem", "space"), check_vma=False)
```

```python
import functools

import jax
import jax.numpy as jnp
from jax import lax
from jax.experimental import pallas as pl
from jax.experimental.pallas import tpu as pltpu
from jax.sharding import PartitionSpec as P

RADIUS = 32768
OFFSETS = (-2, 2, -1, 1)
SLOT = {-2: 0, 0: 1, 2: 2, -1: 3, 1: 4}
CHUNK = 256
SPAN = 512
GROUP = 64
PARTS = 2
f32, bf16 = jnp.float32, jnp.bfloat16


def gather_kernel(idx_ref, state_ref, pos_ref, value_ref, var_ref, out_ref, row_ref):
    half_members, cols = state_ref.shape
    batches, obs_dev = idx_ref.shape
    base = lax.axis_index("space") * cols
    lanes = lax.broadcasted_iota(jnp.int32, (half_members, 128), 1)
    along = lax.broadcasted_iota(jnp.int32, (obs_dev, obs_dev), 1)
    down = lax.broadcasted_iota(jnp.int32, (obs_dev, obs_dev), 0)
    for batch in range(batches):
        parts = []
        for part in range(obs_dev // 128):
            def pick(step, acc):
                for inner in range(32):
                    t = step * 32 + inner
                    col = idx_ref[batch, part * 128 + t] - base
                    hi = lax.shift_right_logical(col, 7)
                    lo = col & 127
                    tile = state_ref[:, pl.ds(pl.multiple_of(hi * 128, 128), 128)]
                    moved = pltpu.roll(tile, (t - lo) & 127, 1)
                    acc = jnp.where(lanes == t, moved, acc)
                return acc
            parts.append(lax.fori_loop(0, 4, pick, jnp.zeros((half_members, 128), f32)))
        q = (pos_ref[batch:batch + 1, :] - base - cols // 2).astype(f32) * (1.0 / RADIUS)
        each = jnp.broadcast_to(q, (obs_dev, obs_dev))
        mine = jnp.transpose(each)
        before = (each < mine) | ((each == mine) & (along < down))
        rank = jnp.sum(jnp.where(before, 1.0, 0.0), axis=1, keepdims=True)
        order = jnp.where(rank == along.astype(f32), 1.0, 0.0)
        rows = jnp.concatenate(
            [jnp.concatenate(parts, axis=1), q, value_ref[batch:batch + 1, :],
             var_ref[batch:batch + 1, :], jnp.zeros((5, obs_dev), f32)], axis=0)
        placed = jnp.dot(
            rows, order, precision=lax.Precision.HIGHEST, preferred_element_type=f32)
        out_ref[:, batch * obs_dev:(batch + 1) * obs_dev] = placed[:half_members]
        row_ref[batch] = placed[half_members:]


def kernel(
    n_space, batches, obs_dev, half_members, cols,
    g_send, state_ref, row_ref, got_ref, awt_out, aw_out, moment_out, c_out,
    g_recv, g_ref, x_send, x_recv,
    pos_own, pos_nb, aw, coef,
    g_sems, x_sems, pos_ssem, pos_rsem, aw_ssem, aw_rsem,
):
    space = lax.axis_index("space")
    mem = lax.axis_index("mem")
    other = 1 - mem
    width = cols // 2
    members = 2 * half_members
    own_start = mem * width
    other_start = other * width
    base = space * cols
    block = cols / RADIUS
    partner = {"mem": other}
    valid = {o: (space + o >= 0) & (space + o < n_space) for o in OFFSETS}

    barrier = pltpu.get_barrier_semaphore()
    pl.semaphore_signal(barrier, inc=1, device_id=partner, device_id_type=pl.DeviceIdType.MESH)
    for o in OFFSETS:
        @pl.when(valid[o])
        def _(o=o):
            pl.semaphore_signal(
                barrier, inc=1, device_id={"space": space + o},
                device_id_type=pl.DeviceIdType.MESH)

    def g_copy(part):
        span = pl.ds(0, obs_dev) if part == 0 else pl.ds(obs_dev, (batches - 1) * obs_dev)
        return pltpu.make_async_remote_copy(
            src_ref=g_send.at[:, span], dst_ref=g_recv.at[:, span],
            send_sem=g_sems.at[0, part], recv_sem=g_sems.at[1, part],
            device_id=partner, device_id_type=pl.DeviceIdType.MESH)

    x_copy = pltpu.make_async_remote_copy(
        src_ref=x_send, dst_ref=x_recv, send_sem=x_sems.at[0], recv_sem=x_sems.at[1],
        device_id=partner, device_id_type=pl.DeviceIdType.MESH)

    def pos_copy(o):
        i = OFFSETS.index(o)
        back = OFFSETS.index(-o)
        return pltpu.make_async_remote_copy(
            src_ref=pos_own, dst_ref=pos_nb.at[back],
            send_sem=pos_ssem.at[i], recv_sem=pos_rsem.at[back],
            device_id={"space": space + o}, device_id_type=pl.DeviceIdType.MESH)

    def pos_wait(o):
        i = OFFSETS.index(o)
        pltpu.make_async_remote_copy(
            src_ref=pos_own, dst_ref=pos_nb.at[i],
            send_sem=pos_ssem.at[i], recv_sem=pos_rsem.at[i],
            device_id={"space": space + o}, device_id_type=pl.DeviceIdType.MESH).wait_recv()

    def aw_copy(batch, o):
        i = OFFSETS.index(o)
        back = OFFSETS.index(-o)
        return pltpu.make_async_remote_copy(
            src_ref=aw.at[batch, SLOT[0]], dst_ref=aw.at[batch, SLOT[-o]],
            send_sem=aw_ssem.at[batch, i], recv_sem=aw_rsem.at[batch, back],
            device_id={"space": space + o}, device_id_type=pl.DeviceIdType.MESH)

    def aw_wait(batch, o):
        i = OFFSETS.index(o)
        pltpu.make_async_remote_copy(
            src_ref=aw.at[batch, SLOT[0]], dst_ref=aw.at[batch, SLOT[o]],
            send_sem=aw_ssem.at[batch, i], recv_sem=aw_rsem.at[batch, i],
            device_id={"space": space + o}, device_id_type=pl.DeviceIdType.MESH).wait_recv()

    pos_own[...] = jnp.zeros_like(pos_own)
    for batch in range(batches):
        pos_own[batch:batch + 1, :] = row_ref[batch, 0:1, :]
    for o in OFFSETS:
        @pl.when(jnp.logical_not(valid[o]))
        def _(o=o):
            pos_nb[OFFSETS.index(o)] = jnp.zeros(pos_nb.shape[1:], f32)
            for batch in range(batches):
                aw[batch, SLOT[o]] = jnp.zeros(aw.shape[2:], bf16)

    count = 1
    for o in OFFSETS:
        count = count + jnp.where(valid[o], 1, 0)
    pl.semaphore_wait(barrier, count)
    g_copy(0).start()
    for o in OFFSETS:
        @pl.when(valid[o])
        def _(o=o):
            pos_copy(o).start()

    def cast(i, carry):
        at = pl.multiple_of(i * 1024, 128)
        x_send[:, pl.ds(at, 1024)] = state_ref[
            :, pl.ds(pl.multiple_of(other_start + at, 128), 1024)].astype(bf16)
        return carry
    lax.fori_loop(0, width // 1024, cast, 0)
    x_copy.start()
    g_copy(1).start()
    g_ref[:half_members, :] = g_send[...]

    def increment(batch, now, u):
        mean = jnp.sum(now, axis=0, keepdims=True) * (1.0 / members)
        anomaly = now - mean
        spread = anomaly.astype(bf16)
        total = jnp.dot(
            moment_out[batch].astype(bf16),
            jnp.concatenate(
                [spread, (anomaly * u).astype(bf16), (anomaly * (u * u)).astype(bf16)], axis=0),
            preferred_element_type=f32)
        for slot in range(3):
            cov = jnp.dot(
                awt_out[batch, slot * obs_dev:(slot + 1) * obs_dev, :members], spread, preferred_element_type=f32)
            c = coef[slot]
            if slot == 0:
                t = jnp.maximum(c - u, 0.0)
            elif slot == 1:
                t = jnp.maximum(1.0 - jnp.abs(c - u), 0.0)
            else:
                t = jnp.maximum(c + u, 0.0)
            gain = (t * t * cov).astype(bf16)
            total = total + jnp.dot(
                aw[batch, slot, members:2 * members, :], gain, preferred_element_type=f32)
        return total

    def build(batch):
        def row(o):
            if o == 0:
                return pos_own[batch:batch + 1, :]
            return pos_nb[OFFSETS.index(o), batch:batch + 1, :] + o * block
        for o in (-2, 0, 2):
            slot = SLOT[o]
            q = row(o)
            c = q if o == 0 else (1.0 + q if o < 0 else 1.0 - q)
            coef[slot] = jnp.transpose(jnp.broadcast_to(c, (CHUNK, obs_dev)))
            c_out[batch, slot:slot + 1, :] = c
            aw_out[batch, slot] = aw[batch, slot]
            awt_out[batch, slot * obs_dev:(slot + 1) * obs_dev, :] = jnp.transpose(
                aw[batch, slot].astype(f32)).astype(bf16)
        sums = 0.0
        for o in (-1, 1):
            slot = SLOT[o]
            q = row(o)
            c = 1.0 + q if o < 0 else 1.0 - q
            a = aw[batch, slot, :members, :].astype(f32)
            rhs = jnp.concatenate([a * (c * c), a * (2.0 * o * c), a], axis=0).astype(bf16)
            sums = sums + lax.dot_general(
                aw[batch, slot, members:2 * members, :], rhs, (((1,), (1,)), ((), ())),
                preferred_element_type=f32)
        moment_out[batch] = sums

    def summarize(batch):
        span = slice(batch * obs_dev, (batch + 1) * obs_dev)
        prior = g_ref[:, span]
        values = row_ref[batch, 1:2, :]
        variances = row_ref[batch, 2:3, :]
        obs_mean = jnp.sum(prior, axis=0, keepdims=True) * (1.0 / members)
        anomaly = prior - obs_mean
        spread = jnp.sum(anomaly * anomaly, axis=0, keepdims=True) * (1.0 / (members - 1)) + 1e-06
        post_var = 1.0 / (1.0 / spread + 1.0 / variances)
        post_mean = post_var * (obs_mean / spread + values / variances)
        change = post_mean - obs_mean + (jnp.sqrt(post_var / spread) - 1.0) * anomaly
        aw[batch, SLOT[0], :members, :] = anomaly.astype(bf16)
        aw[batch, SLOT[0], members:, :] = (change / ((members - 1) * spread)).astype(bf16)

    for batch in range(batches):
        if batch == 0:
            g_copy(0).wait_recv()
            g_ref[half_members:, :obs_dev] = g_recv[:, :obs_dev]
        summarize(batch)
        for o in OFFSETS:
            @pl.when(valid[o])
            def _(o=o):
                aw_copy(batch, o).start()
        if batch == 0:
            g_copy(1).wait_recv()
            g_ref[half_members:, obs_dev:] = g_recv[:, obs_dev:]
            for o in OFFSETS:
                @pl.when(valid[o])
                def _(o=o):
                    pos_wait(o)
        for o in OFFSETS:
            @pl.when(valid[o])
            def _(o=o):
                aw_wait(batch, o)
        build(batch)
        for later in range(batch + 1, batches):
            span = slice(later * obs_dev, (later + 1) * obs_dev)
            now = g_ref[:, span]
            g_ref[:, span] = now + increment(batch, now, pos_own[later:later + 1, :])
    x_copy.wait_recv()
    got_ref[...] = x_recv[...]

    g_copy(0).wait_send()
    g_copy(1).wait_send()
    x_copy.wait_send()
    for o in OFFSETS:
        @pl.when(valid[o])
        def _(o=o):
            pos_copy(o).wait_send()
            for batch in range(batches):
                aw_copy(batch, o).wait_send()


def update_kernel(
    first, bound_ref, state_ref, got_ref, awt_ref, aw_ref, moment_ref, c_ref,
    own_ref, sent_ref, cur, coef,
):
    half_members, cols = state_ref.shape
    batches, _, _, obs_dev = aw_ref.shape
    members = 2 * half_members
    part_width = own_ref.shape[1]
    start = lax.axis_index("mem") * (cols // 2) + first
    chunks = part_width // SPAN
    lane_u = lax.broadcasted_iota(jnp.int32, (1, SPAN), 1)
    index = lax.broadcasted_iota(jnp.int32, (1, obs_dev), 1)

    def span_of(i):
        return pl.ds(pl.multiple_of(i * SPAN, SPAN), SPAN)

    def load(i, carry):
        cur[:half_members, span_of(i)] = state_ref[
            :, pl.ds(pl.multiple_of(start + i * SPAN, SPAN), SPAN)]
        cur[half_members:, span_of(i)] = got_ref[:, span_of(first // SPAN + i)].astype(f32)
        return carry
    lax.fori_loop(0, chunks, load, 0)

    def assimilate(batch, carry):
        for slot in range(3):
            coef[slot] = jnp.transpose(
                jnp.broadcast_to(c_ref[batch, slot:slot + 1, :], (128, obs_dev)))

        def chunk(i, inner):
            now = cur[:, span_of(i)]
            mean = jnp.sum(now, axis=0, keepdims=True) * (1.0 / members)
            anomaly = now - mean
            spread = anomaly.astype(bf16)
            u = (lane_u + (start + i * SPAN - cols // 2)).astype(f32) * (1.0 / RADIUS)
            mix = moment_ref[batch]
            bounds = []
            for slot in range(3):
                at = (slot * 2) * (cols // 2 // SPAN) + first // SPAN + i
                low = bound_ref[batch, at]
                high = bound_ref[batch, at + cols // 2 // SPAN]
                none = low == high
                first_group = low // GROUP
                last_group = jnp.where(none, first_group, (high + GROUP - 1) // GROUP)
                bounds.append((first_group, last_group))
                left = index < jnp.where(none, low, first_group * GROUP)
                right = index >= jnp.where(none, low, last_group * GROUP)
                c = c_ref[batch, slot:slot + 1, :]
                if slot == 0:
                    used, sign = right, -2.0
                elif slot == 1:
                    used = left | right
                    c = jnp.where(left, 1.0 + c, 1.0 - c)
                    sign = jnp.where(left, -2.0, 2.0)
                else:
                    used, sign = left, 2.0
                a = jnp.where(used, aw_ref[batch, slot, :members, :].astype(f32), 0.0)
                rhs = jnp.concatenate([a * (c * c), a * (sign * c), a], axis=0).astype(bf16)
                mix = mix + lax.dot_general(
                    aw_ref[batch, slot, members:, :], rhs, (((1,), (1,)), ((), ())),
                    preferred_element_type=f32)
            total = now + jnp.dot(
                mix.astype(bf16),
                jnp.concatenate(
                    [spread, (anomaly * u).astype(bf16), (anomaly * (u * u)).astype(bf16)],
                    axis=0),
                preferred_element_type=f32)
            cur[:, span_of(i)] = total
            for slot in range(3):
                def dense(g, more):
                    rows = pl.ds(pl.multiple_of(slot * obs_dev + g * GROUP, GROUP), GROUP)
                    pair = awt_ref[batch, rows, :]
                    cov = jnp.dot(pair[:, :members], spread, preferred_element_type=f32)
                    c = coef[slot, pl.ds(pl.multiple_of(g * GROUP, GROUP), GROUP), :]
                    c = jnp.concatenate([c] * (SPAN // 128), axis=1)
                    if slot == 0:
                        t = jnp.maximum(c - u, 0.0)
                    elif slot == 1:
                        t = jnp.maximum(1.0 - jnp.abs(c - u), 0.0)
                    else:
                        t = jnp.maximum(c + u, 0.0)
                    gain = (t * t * cov).astype(bf16)
                    cur[:, span_of(i)] += lax.dot_general(
                        pair[:, members:], gain, (((0,), (0,)), ((), ())),
                        preferred_element_type=f32)
                    return more
                lax.fori_loop(bounds[slot][0], bounds[slot][1], dense, 0)
            return inner
        lax.fori_loop(0, chunks, chunk, 0)
        return carry
    lax.fori_loop(0, batches, assimilate, 0)

    def store(i, carry):
        own_ref[:, span_of(i)] = cur[:half_members, span_of(i)]
        sent_ref[:, span_of(i)] = (
            cur[half_members:, span_of(i)]
            - got_ref[:, span_of(first // SPAN + i)].astype(f32)).astype(bf16)
        return carry
    lax.fori_loop(0, chunks, store, 0)


def shards(n_space, state, obs_index, obs_value, obs_var):
    half_members, cols = state.shape
    batches, obs_dev = obs_index.shape
    members, width = 2 * half_members, cols // 2
    vmem = pl.BlockSpec(memory_space=pltpu.VMEM)
    smem = pl.BlockSpec(memory_space=pltpu.SMEM)
    n_obs = batches * obs_dev
    dma = pltpu.SemaphoreType.DMA
    shape = jax.ShapeDtypeStruct
    gathered, rows = pl.pallas_call(
        gather_kernel,
        out_shape=(shape((half_members, n_obs), f32), shape((batches, 8, obs_dev), f32)),
        in_specs=[smem, vmem, vmem, vmem, vmem],
        out_specs=(vmem, vmem),
        compiler_params=pltpu.CompilerParams(vmem_limit_bytes=32 * 1024 * 1024),
    )(obs_index, state, obs_index, obs_value, obs_var)
    got, awt, aw, moments, c_rows = pl.pallas_call(
        functools.partial(kernel, n_space, batches, obs_dev, half_members, cols),
        out_shape=(
            shape((half_members, width), bf16),
            shape((batches, 3 * obs_dev, 2 * members), bf16),
            shape((batches, 3, 2 * members, obs_dev), bf16),
            shape((batches, members, 3 * members), f32),
            shape((batches, 8, obs_dev), f32),
        ),
        in_specs=[vmem] * 3,
        out_specs=(vmem,) * 5,
        scratch_shapes=[
            pltpu.VMEM((half_members, n_obs), f32),
            pltpu.VMEM((members, n_obs), f32),
            pltpu.VMEM((half_members, width), bf16),
            pltpu.VMEM((half_members, width), bf16),
            pltpu.VMEM((8, obs_dev), f32),
            pltpu.VMEM((4, 8, obs_dev), f32),
            pltpu.VMEM((batches, 5, 2 * members, obs_dev), bf16),
            pltpu.VMEM((3, obs_dev, CHUNK), f32),
            dma((2, 2)), dma((2,)), dma((4,)), dma((4,)),
            dma((batches, 4)), dma((batches, 4)),
        ],
        compiler_params=pltpu.CompilerParams(
            collective_id=0, has_side_effects=True, vmem_limit_bytes=32 * 1024 * 1024),
    )(gathered, state, rows)
    mem = lax.axis_index("mem")
    turn = c_rows[:, :3, :] * jnp.array([1.0, 1.0, -1.0], f32)[None, :, None]
    edges = (mem * width - width + SPAN * lax.iota(jnp.int32, width // SPAN)).astype(f32) / RADIUS
    edges = edges[None, None, :, None]
    low = jnp.sum((turn[:, :, None, :] <= edges).astype(jnp.int32), axis=3)
    high = jnp.sum((turn[:, :, None, :] < edges + (SPAN - 1) / RADIUS).astype(jnp.int32), axis=3)
    bounds = jnp.stack([low, jnp.maximum(low, high)], axis=2).reshape(batches, -1)
    part_width = width // PARTS
    own, come = [], []
    for part in range(PARTS):
        kept, sent = pl.pallas_call(
            functools.partial(update_kernel, part * part_width),
            out_shape=(
                shape((half_members, part_width), f32), shape((half_members, part_width), bf16)),
            in_specs=[smem] + [vmem] * 6,
            out_specs=(vmem, vmem),
            scratch_shapes=[
                pltpu.VMEM((members, part_width), f32), pltpu.VMEM((3, obs_dev, 128), f32)],
            compiler_params=pltpu.CompilerParams(vmem_limit_bytes=32 * 1024 * 1024),
            cost_estimate=pl.CostEstimate(
                flops=12 * 10**9 // PARTS, bytes_accessed=4 * 2**20, transcendentals=0),
        )(bounds, state, got, awt, aw, moments, c_rows)
        own.append(kept)
        come.append(lax.ppermute(sent, "mem", [(0, 1), (1, 0)]))
    own = jnp.concatenate(own, axis=1)
    come = jnp.concatenate(come, axis=1).astype(f32)
    return jnp.where(
        mem == 0,
        jnp.concatenate([own, state[:, width:] + come], axis=1),
        jnp.concatenate([state[:, :width] + come, own], axis=1))


def solution(mesh):
    placed = (P("mem", "space"), P(None, "space"), P(None, "space"), P(None, "space"))
    return jax.shard_map(
        functools.partial(shards, mesh.shape["space"]), mesh=mesh, in_specs=placed,
        out_specs=P("mem", "space"), check_vma=False)
```

```python
import functools

import jax
import jax.numpy as jnp
from jax import lax
from jax.experimental import pallas as pl
from jax.experimental.pallas import tpu as pltpu
from jax.sharding import PartitionSpec as P

RADIUS = 32768
OFFSETS = (-2, 2, -1, 1)
SLOT = {-2: 0, 0: 1, 2: 2, -1: 3, 1: 4}
CHUNK = 256
SPAN = 512
SIDES = ((1, True), (1, False), (0, False), (2, True))
GROUP = 64
PARTS = 2
f32, bf16 = jnp.float32, jnp.bfloat16


def gather_kernel(idx_ref, state_ref, pos_ref, value_ref, var_ref, out_ref, row_ref):
    half_members, cols = state_ref.shape
    batches, obs_dev = idx_ref.shape
    base = lax.axis_index("space") * cols
    lanes = lax.broadcasted_iota(jnp.int32, (half_members, 128), 1)
    along = lax.broadcasted_iota(jnp.int32, (obs_dev, obs_dev), 1)
    down = lax.broadcasted_iota(jnp.int32, (obs_dev, obs_dev), 0)
    for batch in range(batches):
        parts = []
        for part in range(obs_dev // 128):
            def pick(step, acc):
                for inner in range(32):
                    t = step * 32 + inner
                    col = idx_ref[batch, part * 128 + t] - base
                    hi = lax.shift_right_logical(col, 7)
                    lo = col & 127
                    tile = state_ref[:, pl.ds(pl.multiple_of(hi * 128, 128), 128)]
                    moved = pltpu.roll(tile, (t - lo) & 127, 1)
                    acc = jnp.where(lanes == t, moved, acc)
                return acc
            parts.append(lax.fori_loop(0, 4, pick, jnp.zeros((half_members, 128), f32)))
        q = (pos_ref[batch:batch + 1, :] - base - cols // 2).astype(f32) * (1.0 / RADIUS)
        each = jnp.broadcast_to(q, (obs_dev, obs_dev))
        mine = jnp.transpose(each)
        before = (each < mine) | ((each == mine) & (along < down))
        rank = jnp.sum(jnp.where(before, 1.0, 0.0), axis=1, keepdims=True)
        order = jnp.where(rank == along.astype(f32), 1.0, 0.0)
        rows = jnp.concatenate(
            [jnp.concatenate(parts, axis=1), q, value_ref[batch:batch + 1, :],
             var_ref[batch:batch + 1, :], jnp.zeros((5, obs_dev), f32)], axis=0)
        placed = jnp.dot(
            rows, order, precision=lax.Precision.HIGHEST, preferred_element_type=f32)
        out_ref[:, batch * obs_dev:(batch + 1) * obs_dev] = placed[:half_members]
        row_ref[batch] = placed[half_members:]


def kernel(
    n_space, batches, obs_dev, half_members, cols,
    g_send, state_ref, row_ref, got_ref, awt_out, moment_out, c_out,
    g_recv, g_ref, x_send, x_recv,
    pos_own, pos_nb, aw, coef,
    g_sems, x_sems, pos_ssem, pos_rsem, aw_ssem, aw_rsem,
):
    space = lax.axis_index("space")
    mem = lax.axis_index("mem")
    other = 1 - mem
    width = cols // 2
    members = 2 * half_members
    own_start = mem * width
    other_start = other * width
    base = space * cols
    block = cols / RADIUS
    partner = {"mem": other}
    valid = {o: (space + o >= 0) & (space + o < n_space) for o in OFFSETS}

    barrier = pltpu.get_barrier_semaphore()
    pl.semaphore_signal(barrier, inc=1, device_id=partner, device_id_type=pl.DeviceIdType.MESH)
    for o in OFFSETS:
        @pl.when(valid[o])
        def _(o=o):
            pl.semaphore_signal(
                barrier, inc=1, device_id={"space": space + o},
                device_id_type=pl.DeviceIdType.MESH)

    def g_copy(part):
        span = pl.ds(0, obs_dev) if part == 0 else pl.ds(obs_dev, (batches - 1) * obs_dev)
        return pltpu.make_async_remote_copy(
            src_ref=g_send.at[:, span], dst_ref=g_recv.at[:, span],
            send_sem=g_sems.at[0, part], recv_sem=g_sems.at[1, part],
            device_id=partner, device_id_type=pl.DeviceIdType.MESH)

    x_copy = pltpu.make_async_remote_copy(
        src_ref=x_send, dst_ref=x_recv, send_sem=x_sems.at[0], recv_sem=x_sems.at[1],
        device_id=partner, device_id_type=pl.DeviceIdType.MESH)

    def pos_copy(o):
        i = OFFSETS.index(o)
        back = OFFSETS.index(-o)
        return pltpu.make_async_remote_copy(
            src_ref=pos_own, dst_ref=pos_nb.at[back],
            send_sem=pos_ssem.at[i], recv_sem=pos_rsem.at[back],
            device_id={"space": space + o}, device_id_type=pl.DeviceIdType.MESH)

    def pos_wait(o):
        i = OFFSETS.index(o)
        pltpu.make_async_remote_copy(
            src_ref=pos_own, dst_ref=pos_nb.at[i],
            send_sem=pos_ssem.at[i], recv_sem=pos_rsem.at[i],
            device_id={"space": space + o}, device_id_type=pl.DeviceIdType.MESH).wait_recv()

    def aw_copy(batch, o):
        i = OFFSETS.index(o)
        back = OFFSETS.index(-o)
        return pltpu.make_async_remote_copy(
            src_ref=aw.at[batch, SLOT[0]], dst_ref=aw.at[batch, SLOT[-o]],
            send_sem=aw_ssem.at[batch, i], recv_sem=aw_rsem.at[batch, back],
            device_id={"space": space + o}, device_id_type=pl.DeviceIdType.MESH)

    def aw_wait(batch, o):
        i = OFFSETS.index(o)
        pltpu.make_async_remote_copy(
            src_ref=aw.at[batch, SLOT[0]], dst_ref=aw.at[batch, SLOT[o]],
            send_sem=aw_ssem.at[batch, i], recv_sem=aw_rsem.at[batch, i],
            device_id={"space": space + o}, device_id_type=pl.DeviceIdType.MESH).wait_recv()

    pos_own[...] = jnp.zeros_like(pos_own)
    for batch in range(batches):
        pos_own[batch:batch + 1, :] = row_ref[batch, 0:1, :]
    for o in OFFSETS:
        @pl.when(jnp.logical_not(valid[o]))
        def _(o=o):
            pos_nb[OFFSETS.index(o)] = jnp.zeros(pos_nb.shape[1:], f32)
            for batch in range(batches):
                aw[batch, SLOT[o]] = jnp.zeros(aw.shape[2:], bf16)

    count = 1
    for o in OFFSETS:
        count = count + jnp.where(valid[o], 1, 0)
    pl.semaphore_wait(barrier, count)
    g_copy(0).start()
    for o in OFFSETS:
        @pl.when(valid[o])
        def _(o=o):
            pos_copy(o).start()

    def cast(i, carry):
        at = pl.multiple_of(i * 1024, 128)
        x_send[:, pl.ds(at, 1024)] = state_ref[
            :, pl.ds(pl.multiple_of(other_start + at, 128), 1024)].astype(bf16)
        return carry
    lax.fori_loop(0, width // 1024, cast, 0)
    x_copy.start()
    g_copy(1).start()
    g_ref[:half_members, :] = g_send[...]

    def increment(batch, now, u):
        mean = jnp.sum(now, axis=0, keepdims=True) * (1.0 / members)
        anomaly = now - mean
        spread = anomaly.astype(bf16)
        total = jnp.dot(
            moment_out[batch].astype(bf16),
            jnp.concatenate(
                [spread, (anomaly * u).astype(bf16), (anomaly * (u * u)).astype(bf16)], axis=0),
            preferred_element_type=f32)
        for slot in range(3):
            cov = jnp.dot(
                awt_out[batch, slot * obs_dev:(slot + 1) * obs_dev, :members], spread, preferred_element_type=f32)
            c = coef[slot]
            if slot == 0:
                t = jnp.maximum(c - u, 0.0)
            elif slot == 1:
                t = jnp.maximum(1.0 - jnp.abs(c - u), 0.0)
            else:
                t = jnp.maximum(c + u, 0.0)
            gain = (t * t * cov).astype(bf16)
            total = total + jnp.dot(
                aw[batch, slot, members:2 * members, :], gain, preferred_element_type=f32)
        return total

    def build(batch):
        def row(o):
            if o == 0:
                return pos_own[batch:batch + 1, :]
            return pos_nb[OFFSETS.index(o), batch:batch + 1, :] + o * block
        for o in (-2, 0, 2):
            slot = SLOT[o]
            q = row(o)
            c = q if o == 0 else (1.0 + q if o < 0 else 1.0 - q)
            coef[slot] = jnp.transpose(jnp.broadcast_to(c, (CHUNK, obs_dev)))
            c_out[batch, slot:slot + 1, :] = c
            awt_out[batch, slot * obs_dev:(slot + 1) * obs_dev, :] = jnp.transpose(
                aw[batch, slot].astype(f32)).astype(bf16)
        sums = 0.0
        for o in (-1, 1):
            slot = SLOT[o]
            q = row(o)
            c = 1.0 + q if o < 0 else 1.0 - q
            a = aw[batch, slot, :members, :].astype(f32)
            rhs = jnp.concatenate([a * (c * c), a * (2.0 * o * c), a], axis=0).astype(bf16)
            sums = sums + lax.dot_general(
                aw[batch, slot, members:2 * members, :], rhs, (((1,), (1,)), ((), ())),
                preferred_element_type=f32)
        moment_out[batch] = sums

    def summarize(batch):
        span = slice(batch * obs_dev, (batch + 1) * obs_dev)
        prior = g_ref[:, span]
        values = row_ref[batch, 1:2, :]
        variances = row_ref[batch, 2:3, :]
        obs_mean = jnp.sum(prior, axis=0, keepdims=True) * (1.0 / members)
        anomaly = prior - obs_mean
        spread = jnp.sum(anomaly * anomaly, axis=0, keepdims=True) * (1.0 / (members - 1)) + 1e-06
        post_var = 1.0 / (1.0 / spread + 1.0 / variances)
        post_mean = post_var * (obs_mean / spread + values / variances)
        change = post_mean - obs_mean + (jnp.sqrt(post_var / spread) - 1.0) * anomaly
        aw[batch, SLOT[0], :members, :] = anomaly.astype(bf16)
        aw[batch, SLOT[0], members:, :] = (change / ((members - 1) * spread)).astype(bf16)

    for batch in range(batches):
        if batch == 0:
            g_copy(0).wait_recv()
            g_ref[half_members:, :obs_dev] = g_recv[:, :obs_dev]
        summarize(batch)
        for o in OFFSETS:
            @pl.when(valid[o])
            def _(o=o):
                aw_copy(batch, o).start()
        if batch == 0:
            g_copy(1).wait_recv()
            g_ref[half_members:, obs_dev:] = g_recv[:, obs_dev:]
            for o in OFFSETS:
                @pl.when(valid[o])
                def _(o=o):
                    pos_wait(o)
        for o in OFFSETS:
            @pl.when(valid[o])
            def _(o=o):
                aw_wait(batch, o)
        build(batch)
        for later in range(batch + 1, batches):
            span = slice(later * obs_dev, (later + 1) * obs_dev)
            now = g_ref[:, span]
            g_ref[:, span] = now + increment(batch, now, pos_own[later:later + 1, :])
    x_copy.wait_recv()
    got_ref[...] = x_recv[...]

    g_copy(0).wait_send()
    g_copy(1).wait_send()
    x_copy.wait_send()
    for o in OFFSETS:
        @pl.when(valid[o])
        def _(o=o):
            pos_copy(o).wait_send()
            for batch in range(batches):
                aw_copy(batch, o).wait_send()


def update_kernel(
    first, bound_ref, state_ref, got_ref, awt_ref, moment_ref, c_ref,
    own_ref, sent_ref, cur, coef, table,
):
    half_members, cols = state_ref.shape
    batches, obs_dev = c_ref.shape[0], c_ref.shape[2]
    members = 2 * half_members
    part_width = own_ref.shape[1]
    start = lax.axis_index("mem") * (cols // 2) + first
    chunks = part_width // SPAN
    lane_u = lax.broadcasted_iota(jnp.int32, (1, SPAN), 1)
    count = cols // 2 // SPAN
    groups = obs_dev // GROUP

    def span_of(i):
        return pl.ds(pl.multiple_of(i * SPAN, SPAN), SPAN)

    def load(i, carry):
        cur[:half_members, span_of(i)] = state_ref[
            :, pl.ds(pl.multiple_of(start + i * SPAN, SPAN), SPAN)]
        cur[half_members:, span_of(i)] = got_ref[:, span_of(first // SPAN + i)].astype(f32)
        return carry
    lax.fori_loop(0, chunks, load, 0)

    def assimilate(batch, carry):
        for slot in range(3):
            coef[slot] = jnp.transpose(
                jnp.broadcast_to(c_ref[batch, slot:slot + 1, :], (128, obs_dev)))

        for side, (slot, left) in enumerate(SIDES):
            total = moment_ref[batch] if side == 0 else jnp.zeros((members, 3 * members), f32)
            for step in range(groups):
                g = step if left else groups - 1 - step
                table[side, g if left else g + 1] = total
                rows = slice(g * GROUP, (g + 1) * GROUP)
                pair = awt_ref[batch, pl.ds(slot * obs_dev + g * GROUP, GROUP), :]
                a = pair[:, :members].astype(f32)
                c = coef[slot, rows, :members]
                if slot == 1:
                    c = 1.0 + c if left else 1.0 - c
                sign = -2.0 if (slot == 0 or (slot == 1 and left)) else 2.0
                rhs = jnp.concatenate([a * (c * c), a * (sign * c), a], axis=1).astype(bf16)
                total = total + lax.dot_general(
                    pair[:, members:], rhs, (((0,), (0,)), ((), ())),
                    preferred_element_type=f32)
            table[side, groups if left else 0] = total

        def taper_of(slot, c, u):
            c = jnp.concatenate([c] * (SPAN // 128), axis=1)
            if slot == 0:
                t = jnp.maximum(c - u, 0.0)
            elif slot == 1:
                t = jnp.maximum(1.0 - jnp.abs(c - u), 0.0)
            else:
                t = jnp.maximum(c + u, 0.0)
            return t * t

        def chunk(i):
            now = cur[:, span_of(i)]
            mean = jnp.sum(now, axis=0, keepdims=True) * (1.0 / members)
            anomaly = now - mean
            spread = anomaly.astype(bf16)
            u = (lane_u + (start + i * SPAN - cols // 2)).astype(f32) * (1.0 / RADIUS)
            pairs, tapers, bounds = [], [], []
            for slot in range(3):
                at = (slot * 2) * count + first // SPAN + i
                low = jnp.minimum(bound_ref[batch, at] // GROUP, groups - 1)
                high = jnp.maximum(
                    (bound_ref[batch, at + count] + GROUP - 1) // GROUP, low + 1)
                bounds.append((low, high))
                pairs.append(awt_ref[
                    batch, pl.ds(pl.multiple_of(slot * obs_dev + low * GROUP, GROUP), GROUP), :])
                tapers.append(taper_of(
                    slot, coef[slot, pl.ds(pl.multiple_of(low * GROUP, GROUP), GROUP), :], u))
            mix = sum(table[side, bounds[slot][0 if left else 1]]
                      for side, (slot, left) in enumerate(SIDES))
            pair = jnp.concatenate(pairs, axis=0)
            cov = jnp.dot(pair[:, :members], spread, preferred_element_type=f32)
            gain = (jnp.concatenate(tapers, axis=0) * cov).astype(bf16)
            total = now + jnp.dot(
                mix.astype(bf16),
                jnp.concatenate(
                    [spread, (anomaly * u).astype(bf16), (anomaly * (u * u)).astype(bf16)],
                    axis=0),
                preferred_element_type=f32)
            total = total + lax.dot_general(
                pair[:, members:], gain, (((0,), (0,)), ((), ())), preferred_element_type=f32)
            return total, spread, u, bounds

        def more_groups(i, spread, u, bounds):
            for slot in range(3):
                def dense(g, more):
                    rows = pl.ds(pl.multiple_of(slot * obs_dev + g * GROUP, GROUP), GROUP)
                    pair = awt_ref[batch, rows, :]
                    cov = jnp.dot(pair[:, :members], spread, preferred_element_type=f32)
                    c = coef[slot, pl.ds(pl.multiple_of(g * GROUP, GROUP), GROUP), :]
                    gain = (taper_of(slot, c, u) * cov).astype(bf16)
                    cur[:, span_of(i)] += lax.dot_general(
                        pair[:, members:], gain, (((0,), (0,)), ((), ())),
                        preferred_element_type=f32)
                    return more
                lax.fori_loop(bounds[slot][0] + 1, bounds[slot][1], dense, 0)

        def two(step, inner):
            both = [chunk(2 * step + k) for k in range(2)]
            for k in range(2):
                cur[:, span_of(2 * step + k)] = both[k][0]
            for k in range(2):
                more_groups(2 * step + k, *both[k][1:])
            return inner
        lax.fori_loop(0, chunks // 2, two, 0)
        return carry
    lax.fori_loop(0, batches, assimilate, 0)

    def store(i, carry):
        own_ref[:, span_of(i)] = cur[:half_members, span_of(i)]
        sent_ref[:, span_of(i)] = (
            cur[half_members:, span_of(i)]
            - got_ref[:, span_of(first // SPAN + i)].astype(f32)).astype(bf16)
        return carry
    lax.fori_loop(0, chunks, store, 0)


def shards(n_space, state, obs_index, obs_value, obs_var):
    half_members, cols = state.shape
    batches, obs_dev = obs_index.shape
    members, width = 2 * half_members, cols // 2
    vmem = pl.BlockSpec(memory_space=pltpu.VMEM)
    smem = pl.BlockSpec(memory_space=pltpu.SMEM)
    n_obs = batches * obs_dev
    dma = pltpu.SemaphoreType.DMA
    shape = jax.ShapeDtypeStruct
    gathered, rows = pl.pallas_call(
        gather_kernel,
        out_shape=(shape((half_members, n_obs), f32), shape((batches, 8, obs_dev), f32)),
        in_specs=[smem, vmem, vmem, vmem, vmem],
        out_specs=(vmem, vmem),
        compiler_params=pltpu.CompilerParams(vmem_limit_bytes=32 * 1024 * 1024),
    )(obs_index, state, obs_index, obs_value, obs_var)
    got, awt, moments, c_rows = pl.pallas_call(
        functools.partial(kernel, n_space, batches, obs_dev, half_members, cols),
        out_shape=(
            shape((half_members, width), bf16),
            shape((batches, 3 * obs_dev, 2 * members), bf16),
            shape((batches, members, 3 * members), f32),
            shape((batches, 8, obs_dev), f32),
        ),
        in_specs=[vmem] * 3,
        out_specs=(vmem,) * 4,
        scratch_shapes=[
            pltpu.VMEM((half_members, n_obs), f32),
            pltpu.VMEM((members, n_obs), f32),
            pltpu.VMEM((half_members, width), bf16),
            pltpu.VMEM((half_members, width), bf16),
            pltpu.VMEM((8, obs_dev), f32),
            pltpu.VMEM((4, 8, obs_dev), f32),
            pltpu.VMEM((batches, 5, 2 * members, obs_dev), bf16),
            pltpu.VMEM((3, obs_dev, CHUNK), f32),
            dma((2, 2)), dma((2,)), dma((4,)), dma((4,)),
            dma((batches, 4)), dma((batches, 4)),
        ],
        compiler_params=pltpu.CompilerParams(
            collective_id=0, has_side_effects=True, vmem_limit_bytes=32 * 1024 * 1024),
    )(gathered, state, rows)
    mem = lax.axis_index("mem")
    turn = c_rows[:, :3, :] * jnp.array([1.0, 1.0, -1.0], f32)[None, :, None]
    edges = (mem * width - width + SPAN * lax.iota(jnp.int32, width // SPAN)).astype(f32) / RADIUS
    edges = edges[None, None, :, None]
    low = jnp.sum((turn[:, :, None, :] <= edges).astype(jnp.int32), axis=3)
    high = jnp.sum((turn[:, :, None, :] < edges + (SPAN - 1) / RADIUS).astype(jnp.int32), axis=3)
    bounds = jnp.stack([low, jnp.maximum(low, high)], axis=2).reshape(batches, -1)
    part_width = width // PARTS
    own, come = [], []
    for part in range(PARTS):
        kept, sent = pl.pallas_call(
            functools.partial(update_kernel, part * part_width),
            out_shape=(
                shape((half_members, part_width), f32), shape((half_members, part_width), bf16)),
            in_specs=[smem] + [vmem] * 5,
            out_specs=(vmem, vmem),
            scratch_shapes=[
                pltpu.VMEM((members, part_width), f32), pltpu.VMEM((3, obs_dev, 128), f32),
                pltpu.VMEM((4, obs_dev // GROUP + 1, members, 3 * members), f32)],
            compiler_params=pltpu.CompilerParams(vmem_limit_bytes=32 * 1024 * 1024),
            cost_estimate=pl.CostEstimate(
                flops=12 * 10**9 // PARTS, bytes_accessed=4 * 2**20, transcendentals=0),
        )(bounds, state, got, awt, moments, c_rows)
        own.append(kept)
        come.append(lax.ppermute(sent, "mem", [(0, 1), (1, 0)]))
    own = jnp.concatenate(own, axis=1)
    come = jnp.concatenate(come, axis=1).astype(f32)
    return jnp.where(
        mem == 0,
        jnp.concatenate([own, state[:, width:] + come], axis=1),
        jnp.concatenate([state[:, :width] + come, own], axis=1))


def solution(mesh):
    placed = (P("mem", "space"), P(None, "space"), P(None, "space"), P(None, "space"))
    return jax.shard_map(
        functools.partial(shards, mesh.shape["space"]), mesh=mesh, in_specs=placed,
        out_specs=P("mem", "space"), check_vma=False)
```

```python
import functools

import jax
import jax.numpy as jnp
from jax import lax
from jax.experimental import pallas as pl
from jax.experimental.pallas import tpu as pltpu
from jax.sharding import PartitionSpec as P

RADIUS = 32768
OFFSETS = (-2, 2, -1, 1)
SLOT = {-2: 0, 0: 1, 2: 2, -1: 3, 1: 4}
CHUNK = 256
SPAN = 512
SIDES = ((1, True), (1, False), (0, False), (2, True))
GROUP = 64
PARTS = (3, 1)
f32, bf16 = jnp.float32, jnp.bfloat16


def gather_kernel(
    idx_ref, state_ref, pos_any, value_any, var_any, out_ref, row_ref,
    pos_ref, value_ref, var_ref, sems,
):
    copies = [
        pltpu.make_async_copy(src, dst, sems.at[i])
        for i, (src, dst) in enumerate(
            ((pos_any, pos_ref), (value_any, value_ref), (var_any, var_ref)))
    ]
    for copy in copies:
        copy.start()
    half_members, cols = state_ref.shape
    batches, obs_dev = idx_ref.shape
    base = lax.axis_index("space") * cols
    lanes = lax.broadcasted_iota(jnp.int32, (half_members, 128), 1)
    along = lax.broadcasted_iota(jnp.int32, (obs_dev, obs_dev), 1)
    down = lax.broadcasted_iota(jnp.int32, (obs_dev, obs_dev), 0)
    for batch in range(batches):
        parts = []
        for part in range(obs_dev // 128):
            def pick(step, acc):
                for inner in range(32):
                    t = step * 32 + inner
                    col = idx_ref[batch, part * 128 + t] - base
                    hi = lax.shift_right_logical(col, 7)
                    lo = col & 127
                    tile = state_ref[:, pl.ds(pl.multiple_of(hi * 128, 128), 128)]
                    moved = pltpu.roll(tile, (t - lo) & 127, 1)
                    acc = jnp.where(lanes == t, moved, acc)
                return acc
            parts.append(lax.fori_loop(0, 4, pick, jnp.zeros((half_members, 128), f32)))
        if batch == 0:
            for copy in copies:
                copy.wait()
        q = (pos_ref[batch:batch + 1, :] - base - cols // 2).astype(f32) * (1.0 / RADIUS)
        each = jnp.broadcast_to(q, (obs_dev, obs_dev))
        mine = jnp.transpose(each)
        before = (each < mine) | ((each == mine) & (along < down))
        rank = jnp.sum(jnp.where(before, 1.0, 0.0), axis=1, keepdims=True)
        order = jnp.where(rank == along.astype(f32), 1.0, 0.0)
        rows = jnp.concatenate(
            [jnp.concatenate(parts, axis=1), q, value_ref[batch:batch + 1, :],
             var_ref[batch:batch + 1, :], jnp.zeros((5, obs_dev), f32)], axis=0)
        placed = jnp.dot(
            rows, order, precision=lax.Precision.HIGHEST, preferred_element_type=f32)
        out_ref[:, batch * obs_dev:(batch + 1) * obs_dev] = placed[:half_members]
        row_ref[batch] = placed[half_members:]


def kernel(
    n_space, batches, obs_dev, half_members, cols,
    g_send, state_ref, row_ref, got_ref, awt_out, moment_out, c_out,
    g_recv, g_ref, x_send, x_recv,
    pos_own, pos_nb, aw, coef,
    g_sems, x_sems, pos_ssem, pos_rsem, aw_ssem, aw_rsem,
):
    space = lax.axis_index("space")
    mem = lax.axis_index("mem")
    other = 1 - mem
    width = cols // 2
    members = 2 * half_members
    own_start = mem * width
    other_start = other * width
    base = space * cols
    block = cols / RADIUS
    partner = {"mem": other}
    valid = {o: (space + o >= 0) & (space + o < n_space) for o in OFFSETS}

    barrier = pltpu.get_barrier_semaphore()
    pl.semaphore_signal(barrier, inc=1, device_id=partner, device_id_type=pl.DeviceIdType.MESH)
    for o in OFFSETS:
        @pl.when(valid[o])
        def _(o=o):
            pl.semaphore_signal(
                barrier, inc=1, device_id={"space": space + o},
                device_id_type=pl.DeviceIdType.MESH)

    def g_copy(part):
        span = pl.ds(0, obs_dev) if part == 0 else pl.ds(obs_dev, (batches - 1) * obs_dev)
        return pltpu.make_async_remote_copy(
            src_ref=g_send.at[:, span], dst_ref=g_recv.at[:, span],
            send_sem=g_sems.at[0, part], recv_sem=g_sems.at[1, part],
            device_id=partner, device_id_type=pl.DeviceIdType.MESH)

    x_copy = pltpu.make_async_remote_copy(
        src_ref=x_send, dst_ref=x_recv, send_sem=x_sems.at[0], recv_sem=x_sems.at[1],
        device_id=partner, device_id_type=pl.DeviceIdType.MESH)

    def pos_copy(o):
        i = OFFSETS.index(o)
        back = OFFSETS.index(-o)
        return pltpu.make_async_remote_copy(
            src_ref=pos_own, dst_ref=pos_nb.at[back],
            send_sem=pos_ssem.at[i], recv_sem=pos_rsem.at[back],
            device_id={"space": space + o}, device_id_type=pl.DeviceIdType.MESH)

    def pos_wait(o):
        i = OFFSETS.index(o)
        pltpu.make_async_remote_copy(
            src_ref=pos_own, dst_ref=pos_nb.at[i],
            send_sem=pos_ssem.at[i], recv_sem=pos_rsem.at[i],
            device_id={"space": space + o}, device_id_type=pl.DeviceIdType.MESH).wait_recv()

    def aw_copy(batch, o):
        i = OFFSETS.index(o)
        back = OFFSETS.index(-o)
        return pltpu.make_async_remote_copy(
            src_ref=aw.at[batch, SLOT[0]], dst_ref=aw.at[batch, SLOT[-o]],
            send_sem=aw_ssem.at[batch, i], recv_sem=aw_rsem.at[batch, back],
            device_id={"space": space + o}, device_id_type=pl.DeviceIdType.MESH)

    def aw_wait(batch, o):
        i = OFFSETS.index(o)
        pltpu.make_async_remote_copy(
            src_ref=aw.at[batch, SLOT[0]], dst_ref=aw.at[batch, SLOT[o]],
            send_sem=aw_ssem.at[batch, i], recv_sem=aw_rsem.at[batch, i],
            device_id={"space": space + o}, device_id_type=pl.DeviceIdType.MESH).wait_recv()

    pos_own[...] = jnp.zeros_like(pos_own)
    for batch in range(batches):
        pos_own[batch:batch + 1, :] = row_ref[batch, 0:1, :]
    for o in OFFSETS:
        @pl.when(jnp.logical_not(valid[o]))
        def _(o=o):
            pos_nb[OFFSETS.index(o)] = jnp.zeros(pos_nb.shape[1:], f32)
            for batch in range(batches):
                aw[batch, SLOT[o]] = jnp.zeros(aw.shape[2:], bf16)

    count = 1
    for o in OFFSETS:
        count = count + jnp.where(valid[o], 1, 0)
    pl.semaphore_wait(barrier, count)
    g_copy(0).start()
    for o in OFFSETS:
        @pl.when(valid[o])
        def _(o=o):
            pos_copy(o).start()

    def cast(i, carry):
        at = pl.multiple_of(i * 1024, 128)
        x_send[:, pl.ds(at, 1024)] = state_ref[
            :, pl.ds(pl.multiple_of(other_start + at, 128), 1024)].astype(bf16)
        return carry
    lax.fori_loop(0, width // 1024, cast, 0)
    x_copy.start()
    g_copy(1).start()
    g_ref[:half_members, :] = g_send[...]

    def increment(batch, now, u):
        mean = jnp.sum(now, axis=0, keepdims=True) * (1.0 / members)
        anomaly = now - mean
        spread = anomaly.astype(bf16)
        total = jnp.dot(
            moment_out[batch].astype(bf16),
            jnp.concatenate(
                [spread, (anomaly * u).astype(bf16), (anomaly * (u * u)).astype(bf16)], axis=0),
            preferred_element_type=f32)
        for slot in range(3):
            cov = jnp.dot(
                awt_out[batch, slot * obs_dev:(slot + 1) * obs_dev, :members], spread, preferred_element_type=f32)
            c = coef[slot]
            if slot == 0:
                t = jnp.maximum(c - u, 0.0)
            elif slot == 1:
                t = jnp.maximum(1.0 - jnp.abs(c - u), 0.0)
            else:
                t = jnp.maximum(c + u, 0.0)
            gain = (t * t * cov).astype(bf16)
            total = total + jnp.dot(
                aw[batch, slot, members:2 * members, :], gain, preferred_element_type=f32)
        return total

    def row(batch, o):
        if o == 0:
            return pos_own[batch:batch + 1, :]
        return pos_nb[OFFSETS.index(o), batch:batch + 1, :] + o * block

    def turn_around(batch, slot):
        awt_out[batch, slot * obs_dev:(slot + 1) * obs_dev, :] = jnp.transpose(
            aw[batch, slot].astype(f32)).astype(bf16)

    def build_early(batch):
        for o in (-2, 0, 2):
            slot = SLOT[o]
            q = row(batch, o)
            c = q if o == 0 else (1.0 + q if o < 0 else 1.0 - q)
            coef[slot] = jnp.transpose(jnp.broadcast_to(c, (CHUNK, obs_dev)))
            c_out[batch, slot:slot + 1, :] = c
        turn_around(batch, SLOT[0])

    def build(batch):
        turn_around(batch, SLOT[-2])
        turn_around(batch, SLOT[2])
        sums = 0.0
        for o in (-1, 1):
            slot = SLOT[o]
            q = row(batch, o)
            c = 1.0 + q if o < 0 else 1.0 - q
            a = aw[batch, slot, :members, :].astype(f32)
            rhs = jnp.concatenate([a * (c * c), a * (2.0 * o * c), a], axis=0).astype(bf16)
            sums = sums + lax.dot_general(
                aw[batch, slot, members:2 * members, :], rhs, (((1,), (1,)), ((), ())),
                preferred_element_type=f32)
        moment_out[batch] = sums

    def summarize(batch):
        span = slice(batch * obs_dev, (batch + 1) * obs_dev)
        prior = g_ref[:, span]
        values = row_ref[batch, 1:2, :]
        variances = row_ref[batch, 2:3, :]
        obs_mean = jnp.sum(prior, axis=0, keepdims=True) * (1.0 / members)
        anomaly = prior - obs_mean
        spread = jnp.sum(anomaly * anomaly, axis=0, keepdims=True) * (1.0 / (members - 1)) + 1e-06
        post_var = 1.0 / (1.0 / spread + 1.0 / variances)
        post_mean = post_var * (obs_mean / spread + values / variances)
        change = post_mean - obs_mean + (jnp.sqrt(post_var / spread) - 1.0) * anomaly
        aw[batch, SLOT[0], :members, :] = anomaly.astype(bf16)
        aw[batch, SLOT[0], members:, :] = (change / ((members - 1) * spread)).astype(bf16)

    def advance(batch, later):
        if batch < 0:
            return
        span = slice(later * obs_dev, (later + 1) * obs_dev)
        now = g_ref[:, span]
        g_ref[:, span] = now + increment(batch, now, pos_own[later:later + 1, :])

    for batch in range(batches):
        if batch == 0:
            g_copy(0).wait_recv()
            g_ref[half_members:, :obs_dev] = g_recv[:, :obs_dev]
        summarize(batch)
        for o in OFFSETS:
            @pl.when(valid[o])
            def _(o=o):
                aw_copy(batch, o).start()
        if batch == 0:
            g_copy(1).wait_recv()
            g_ref[half_members:, obs_dev:] = g_recv[:, obs_dev:]
            for o in OFFSETS:
                @pl.when(valid[o])
                def _(o=o):
                    pos_wait(o)
        for later in range(batch + 1, batches):
            advance(batch - 1, later)
        build_early(batch)
        for o in OFFSETS:
            @pl.when(valid[o])
            def _(o=o):
                aw_wait(batch, o)
        build(batch)
        if batch + 1 < batches:
            advance(batch, batch + 1)
    x_copy.wait_recv()
    got_ref[...] = x_recv[...]

    g_copy(0).wait_send()
    g_copy(1).wait_send()
    x_copy.wait_send()
    for o in OFFSETS:
        @pl.when(valid[o])
        def _(o=o):
            pos_copy(o).wait_send()
            for batch in range(batches):
                aw_copy(batch, o).wait_send()


def update_kernel(
    first, bound_ref, state_ref, got_ref, awt_ref, moment_ref, c_ref,
    own_ref, sent_ref, cur, coef, table,
):
    half_members, cols = state_ref.shape
    batches, obs_dev = c_ref.shape[0], c_ref.shape[2]
    members = 2 * half_members
    part_width = own_ref.shape[1]
    start = lax.axis_index("mem") * (cols // 2) + first
    chunks = part_width // SPAN
    lane_u = lax.broadcasted_iota(jnp.int32, (1, SPAN), 1)
    count = cols // 2 // SPAN
    groups = obs_dev // GROUP

    def span_of(i):
        return pl.ds(pl.multiple_of(i * SPAN, SPAN), SPAN)

    def load(i, carry):
        cur[:half_members, span_of(i)] = state_ref[
            :, pl.ds(pl.multiple_of(start + i * SPAN, SPAN), SPAN)]
        cur[half_members:, span_of(i)] = got_ref[:, span_of(first // SPAN + i)].astype(f32)
        return carry
    lax.fori_loop(0, chunks, load, 0)

    def assimilate(batch, carry):
        for slot in range(3):
            coef[slot] = jnp.transpose(
                jnp.broadcast_to(c_ref[batch, slot:slot + 1, :], (128, obs_dev)))

        for side, (slot, left) in enumerate(SIDES):
            total = moment_ref[batch] if side == 0 else jnp.zeros((members, 3 * members), f32)
            for step in range(groups):
                g = step if left else groups - 1 - step
                table[side, g if left else g + 1] = total
                rows = slice(g * GROUP, (g + 1) * GROUP)
                pair = awt_ref[batch, pl.ds(slot * obs_dev + g * GROUP, GROUP), :]
                a = pair[:, :members].astype(f32)
                c = coef[slot, rows, :members]
                if slot == 1:
                    c = 1.0 + c if left else 1.0 - c
                sign = -2.0 if (slot == 0 or (slot == 1 and left)) else 2.0
                rhs = jnp.concatenate([a * (c * c), a * (sign * c), a], axis=1).astype(bf16)
                total = total + lax.dot_general(
                    pair[:, members:], rhs, (((0,), (0,)), ((), ())),
                    preferred_element_type=f32)
            table[side, groups if left else 0] = total

        def taper_of(slot, c, u):
            c = jnp.concatenate([c] * (SPAN // 128), axis=1)
            if slot == 0:
                t = jnp.maximum(c - u, 0.0)
            elif slot == 1:
                t = jnp.maximum(1.0 - jnp.abs(c - u), 0.0)
            else:
                t = jnp.maximum(c + u, 0.0)
            return t * t

        def chunk(i):
            now = cur[:, span_of(i)]
            mean = jnp.sum(now, axis=0, keepdims=True) * (1.0 / members)
            anomaly = now - mean
            spread = anomaly.astype(bf16)
            u = (lane_u + (start + i * SPAN - cols // 2)).astype(f32) * (1.0 / RADIUS)
            pairs, tapers, bounds = [], [], []
            for slot in range(3):
                at = (slot * 2) * count + first // SPAN + i
                low = jnp.minimum(bound_ref[batch, at] // GROUP, groups - 1)
                high = jnp.maximum(
                    (bound_ref[batch, at + count] + GROUP - 1) // GROUP, low + 1)
                bounds.append((low, high))
                pairs.append(awt_ref[
                    batch, pl.ds(pl.multiple_of(slot * obs_dev + low * GROUP, GROUP), GROUP), :])
                tapers.append(taper_of(
                    slot, coef[slot, pl.ds(pl.multiple_of(low * GROUP, GROUP), GROUP), :], u))
            mix = sum(table[side, bounds[slot][0 if left else 1]]
                      for side, (slot, left) in enumerate(SIDES))
            pair = jnp.concatenate(pairs, axis=0)
            cov = jnp.dot(pair[:, :members], spread, preferred_element_type=f32)
            gain = (jnp.concatenate(tapers, axis=0) * cov).astype(bf16)
            total = now + jnp.dot(
                mix.astype(bf16),
                jnp.concatenate(
                    [spread, (anomaly * u).astype(bf16), (anomaly * (u * u)).astype(bf16)],
                    axis=0),
                preferred_element_type=f32)
            total = total + lax.dot_general(
                pair[:, members:], gain, (((0,), (0,)), ((), ())), preferred_element_type=f32)
            return total, spread, u, bounds

        def more_groups(i, spread, u, bounds):
            for slot in range(3):
                def dense(g, more):
                    rows = pl.ds(pl.multiple_of(slot * obs_dev + g * GROUP, GROUP), GROUP)
                    pair = awt_ref[batch, rows, :]
                    cov = jnp.dot(pair[:, :members], spread, preferred_element_type=f32)
                    c = coef[slot, pl.ds(pl.multiple_of(g * GROUP, GROUP), GROUP), :]
                    gain = (taper_of(slot, c, u) * cov).astype(bf16)
                    cur[:, span_of(i)] += lax.dot_general(
                        pair[:, members:], gain, (((0,), (0,)), ((), ())),
                        preferred_element_type=f32)
                    return more
                lax.fori_loop(bounds[slot][0] + 1, bounds[slot][1], dense, 0)

        def two(step, inner):
            both = [chunk(2 * step + k) for k in range(2)]
            for k in range(2):
                cur[:, span_of(2 * step + k)] = both[k][0]
            for k in range(2):
                more_groups(2 * step + k, *both[k][1:])
            return inner
        lax.fori_loop(0, chunks // 2, two, 0)
        return carry
    lax.fori_loop(0, batches, assimilate, 0)

    def store(i, carry):
        own_ref[:, span_of(i)] = cur[:half_members, span_of(i)]
        sent_ref[:, span_of(i)] = (
            cur[half_members:, span_of(i)]
            - got_ref[:, span_of(first // SPAN + i)].astype(f32)).astype(bf16)
        return carry
    lax.fori_loop(0, chunks, store, 0)


def shards(n_space, state, obs_index, obs_value, obs_var):
    half_members, cols = state.shape
    batches, obs_dev = obs_index.shape
    members, width = 2 * half_members, cols // 2
    vmem = pl.BlockSpec(memory_space=pltpu.VMEM)
    smem = pl.BlockSpec(memory_space=pltpu.SMEM)
    n_obs = batches * obs_dev
    dma = pltpu.SemaphoreType.DMA
    shape = jax.ShapeDtypeStruct
    gathered, rows = pl.pallas_call(
        gather_kernel,
        out_shape=(shape((half_members, n_obs), f32), shape((batches, 8, obs_dev), f32)),
        in_specs=[smem, vmem] + [pl.BlockSpec(memory_space=pl.ANY)] * 3,
        out_specs=(vmem, vmem),
        scratch_shapes=[
            pltpu.VMEM((batches, obs_dev), jnp.int32), pltpu.VMEM((batches, obs_dev), f32),
            pltpu.VMEM((batches, obs_dev), f32), dma((3,)),
        ],
        compiler_params=pltpu.CompilerParams(vmem_limit_bytes=32 * 1024 * 1024),
    )(obs_index, state, obs_index, obs_value, obs_var)
    got, awt, moments, c_rows = pl.pallas_call(
        functools.partial(kernel, n_space, batches, obs_dev, half_members, cols),
        out_shape=(
            shape((half_members, width), bf16),
            shape((batches, 3 * obs_dev, 2 * members), bf16),
            shape((batches, members, 3 * members), f32),
            shape((batches, 8, obs_dev), f32),
        ),
        in_specs=[vmem] * 3,
        out_specs=(vmem,) * 4,
        scratch_shapes=[
            pltpu.VMEM((half_members, n_obs), f32),
            pltpu.VMEM((members, n_obs), f32),
            pltpu.VMEM((half_members, width), bf16),
            pltpu.VMEM((half_members, width), bf16),
            pltpu.VMEM((8, obs_dev), f32),
            pltpu.VMEM((4, 8, obs_dev), f32),
            pltpu.VMEM((batches, 5, 2 * members, obs_dev), bf16),
            pltpu.VMEM((3, obs_dev, CHUNK), f32),
            dma((2, 2)), dma((2,)), dma((4,)), dma((4,)),
            dma((batches, 4)), dma((batches, 4)),
        ],
        compiler_params=pltpu.CompilerParams(
            collective_id=0, has_side_effects=True, vmem_limit_bytes=32 * 1024 * 1024),
    )(gathered, state, rows)
    mem = lax.axis_index("mem")
    turn = c_rows[:, :3, :] * jnp.array([1.0, 1.0, -1.0], f32)[None, :, None]
    edges = (mem * width - width + SPAN * lax.iota(jnp.int32, width // SPAN)).astype(f32) / RADIUS
    edges = edges[None, None, :, None]
    low = jnp.sum((turn[:, :, None, :] <= edges).astype(jnp.int32), axis=3)
    high = jnp.sum((turn[:, :, None, :] < edges + (SPAN - 1) / RADIUS).astype(jnp.int32), axis=3)
    bounds = jnp.stack([low, jnp.maximum(low, high)], axis=2).reshape(batches, -1)
    own, come = [], []
    first = 0
    for part in PARTS:
        part_width = width * part // sum(PARTS)
        kept, sent = pl.pallas_call(
            functools.partial(update_kernel, first),
            out_shape=(
                shape((half_members, part_width), f32), shape((half_members, part_width), bf16)),
            in_specs=[smem] + [vmem] * 5,
            out_specs=(vmem, vmem),
            scratch_shapes=[
                pltpu.VMEM((members, part_width), f32), pltpu.VMEM((3, obs_dev, 128), f32),
                pltpu.VMEM((4, obs_dev // GROUP + 1, members, 3 * members), f32)],
            compiler_params=pltpu.CompilerParams(vmem_limit_bytes=32 * 1024 * 1024),
            cost_estimate=pl.CostEstimate(
                flops=12 * 10**9 * part // sum(PARTS), bytes_accessed=4 * 2**20, transcendentals=0),
        )(bounds, state, got, awt, moments, c_rows)
        first += part_width
        own.append(kept)
        come.append(lax.ppermute(sent, "mem", [(0, 1), (1, 0)]))
    own = jnp.concatenate(own, axis=1)
    come = jnp.concatenate(come, axis=1).astype(f32)
    return jnp.where(
        mem == 0,
        jnp.concatenate([own, state[:, width:] + come], axis=1),
        jnp.concatenate([state[:, :width] + come, own], axis=1))


def solution(mesh):
    placed = (P("mem", "space"), P(None, "space"), P(None, "space"), P(None, "space"))
    return jax.shard_map(
        functools.partial(shards, mesh.shape["space"]), mesh=mesh, in_specs=placed,
        out_specs=P("mem", "space"), check_vma=False)
```
